32 devices in a mesh: cfg: 2 (over y), tm: 4 (over z), space: 2 (over x), spin: 2 (over core).
Axes of the slice: x: 2, y: 2, z: 4, core: 2. Of those that a mesh axis runs over, the one named last changes fastest.
Arguments:
- eigenvectors: bfloat16 [16, 2048, 3, 128], P(('cfg', 'tm'), ('space', 'spin')), parts along dimension 0, may hold values from -1.25 to 1.25
- momenta: int32 [8, 3], replicated, may hold values from -2 to 2, as said below
- time_pairs: int32 [32, 2], P(('cfg', 'tm')), parts along dimension 0, may hold values from 0 to 7
- slot_map: int32 [8], replicated, may hold values from 0 to 7, each once
- perambulators: bfloat16 [32, 64, 2048], P(('cfg', 'tm')), parts along dimension 0, may hold values from -0.046875 to 0.046875
Outputs:
- meson_loops: bfloat16 [32, 8, 64, 16, 128], P(('cfg', 'tm'), None, ('space', 'spin')), parts along dimension 0
The draws below stay inside these ranges and needn't reach their ends.
There are 2 independent parts, one for each index of `cfg`. The reference program is written for one: setup_inputs(seed, part) draws one part's arguments, and reference() takes and returns one part's arrays. A program takes and returns all parts, laid end to end along the dimension named above; an argument that names none is the same for every part. Nothing has to cross between parts.
Inputs may be any that keep to these rules, and one draw needn't show every extreme that they name: `momenta`: every momentum row has a component that is not zero. slot_map is a permutation of the 8 stored rows.
All inputs are finite; a program needn't handle non-finite values.
Results may differ from the reference program's by a relative error of at most 0.0074.
Values may be sent and summed in bfloat16 or wider, within the bound.
A program may use at most 64 MiB of HBM per device.

```python
import jax
import jax.numpy as jnp
from jax import lax

NEV = 64
NMOM = 8
LAT = 32
SITES = 2048
NT = 8
PAIRS = 16


def draw_momenta(key, part):
    values = jax.random.randint(jax.random.fold_in(key, 11), (NMOM, 3), -2, 3).astype(jnp.int32)
    silent = jnp.all(values == 0, axis=1)
    bumped = jnp.where(silent, 1, 0).astype(jnp.int32)
    return values.at[:, 0].add(bumped)


def plant(array, own_key, low, top_value):
    index_at = [jax.random.randint(jax.random.fold_in(own_key, axis), (), 0, length) for axis, length in enumerate(array.shape)]
    widest = array.shape.index(max(array.shape))
    neighbour = index_at[:widest] + [(index_at[widest] + 1) % array.shape[widest]] + index_at[widest + 1:]
    return array.at[tuple(index_at)].set(low).at[tuple(neighbour)].set(top_value)


def levels(own_key, shape, shards, smallest, largest):
    factor_of = 1.0
    for position, blocks in shards:
        steps = jax.random.uniform(jax.random.fold_in(jax.random.fold_in(own_key, 6), position), (blocks,), jnp.float32, smallest / len(shards), largest / len(shards))
        factor_of = factor_of * jnp.repeat(jnp.exp(steps), shape[position] // blocks).reshape((-1,) + (1,) * (len(shape) - 1 - position))
    return factor_of


def normal_values(rng, extent, deviation, most, cuts=(), held_as=jnp.bfloat16):
    gain = levels(rng, extent, cuts, -0.22, 0.18) if cuts else 1.0
    array = jax.random.normal(rng, extent, jnp.float32) * deviation * gain
    return jnp.minimum(jnp.maximum(array, -most), most).astype(held_as)


def setup_inputs(seed: int = 0, part: int = 0) -> dict:
    key_list = jax.random.split(jax.random.key(seed), 6)
    part_splits = jax.random.split(jax.random.fold_in(key_list[5], part), 6)
    eigenvectors = normal_values(part_splits[0], (NT, SITES, 3, 2 * NEV), (1.0 / (12 * SITES) ** 0.25), 1.25, ((0, 4), (1, 4)))
    momenta = draw_momenta(jax.random.fold_in(key_list[5], 71), part)
    time_pairs = plant(jax.random.randint(part_splits[2], (PAIRS, 2), 0, NT), jax.random.fold_in(part_splits[2], 1), 0, NT - 1).astype(jnp.int32)
    slot_map = jax.random.permutation(key_list[3], NT).astype(jnp.int32)
    perambulators = normal_values(part_splits[4], (PAIRS, NEV, 32 * NEV), (4 * NEV * NEV) ** -0.5, 0.046875, ((0, 4),))
    return dict(eigenvectors=eigenvectors, momenta=momenta, time_pairs=time_pairs, slot_map=slot_map, perambulators=perambulators)


TURN = 6.283185307179586


def elemental(time_slab, momenta, first_site):
    site_count = time_slab.shape[0]
    vectors = time_slab.shape[2] // 2
    site_ids = first_site + lax.iota(jnp.int32, site_count)
    coord_x = site_ids % LAT
    coord_y = (site_ids // LAT) % LAT
    coord_z = site_ids // (LAT * LAT)
    real_part = time_slab[:, :, :vectors].astype(jnp.float32)
    imag_part = time_slab[:, :, vectors:].astype(jnp.float32)
    conj_left = time_slab.reshape(site_count * 6, vectors)
    results = []
    for momentum_row in range(momenta.shape[0]):
        wavenum = jnp.mod(momenta[momentum_row, 0] * coord_x + momenta[momentum_row, 1] * coord_y + momenta[momentum_row, 2] * coord_z, LAT)
        angles = wavenum.astype(jnp.float32) * (TURN / LAT)
        cosine = jnp.cos(angles)[:, None, None]
        sines = jnp.sin(angles)[:, None, None]
        turned_real = cosine * real_part - sines * imag_part
        turned_imag = sines * real_part + cosine * imag_part
        upper_rows = jnp.concatenate([turned_real, turned_imag], axis=-1)
        lower_rows = jnp.concatenate([turned_imag, -turned_real], axis=-1)
        phased = jnp.stack([upper_rows, lower_rows], axis=2).reshape(site_count * 6, 2 * vectors).astype(jnp.bfloat16)
        results.append(jnp.dot(conj_left.T, phased, preferred_element_type=jnp.float32))
    return jnp.stack(results)


def one_pair(inputs):
    sink_block, source_block, tau = inputs
    vectors = tau.shape[0]
    moms = sink_block.shape[0]
    share_rows = sink_block.shape[1]
    parts = tau.reshape(vectors, 16, 2, vectors)
    lower = jnp.stack([-parts[:, :, 1], parts[:, :, 0]], axis=2).reshape(vectors, 32 * vectors)
    right_side = jnp.concatenate([tau, lower], axis=0)
    left_side = sink_block.reshape(moms * share_rows, 2 * vectors)
    halfway = jnp.dot(left_side.astype(jnp.float32), right_side.astype(jnp.float32)).astype(jnp.bfloat16)
    halfway = halfway.reshape(moms, share_rows * 16, 2 * vectors)
    source_parts = source_block.reshape(moms, vectors, 2, vectors)
    swapped = jnp.stack([-source_parts[:, :, 1], source_parts[:, :, 0]], axis=2).reshape(moms, vectors, 2 * vectors)
    conjugate = jnp.stack([source_block, swapped], axis=1).reshape(moms, 2 * vectors, 2 * vectors)
    loops = jnp.einsum("pmx,pnx->pmn", halfway.astype(jnp.float32), conjugate.astype(jnp.float32))
    return loops.astype(jnp.bfloat16).reshape(moms, share_rows, 16, 2 * vectors)


def reference(eigenvectors, momenta, time_pairs, slot_map, perambulators):
    summed = lax.map(lambda time_slab: elemental(time_slab, momenta, 0), eigenvectors)
    elements = summed.astype(jnp.bfloat16)
    sink_full = elements[slot_map[time_pairs[:, 0]]]
    source_full = elements[slot_map[time_pairs[:, 1]]]
    return lax.map(one_pair, (sink_full, source_full, perambulators))
```

```python
import functools

import jax
import jax.numpy as jnp
from jax import lax
from jax.experimental import pallas as pl
from jax.experimental.pallas import tpu as pltpu
from jax.sharding import PartitionSpec as P

LAT = 32
TURN = 6.283185307179586
BF16 = jnp.bfloat16
F32 = jnp.float32
MESH = pl.DeviceIdType.MESH


def phase_tables(momenta, first_site, site_count, moms):
    shape = (site_count, 128)
    lane = lax.broadcasted_iota(jnp.int32, (1, 128), 1)
    rows = []
    for axis in range(3):
        row = jnp.zeros((1, 128), jnp.int32)
        for m in range(moms):
            row = jnp.where(lane == m, momenta[axis, m], row)
        rows.append(row)
    site = first_site + lax.broadcasted_iota(jnp.int32, shape, 0)
    coord_x = lax.rem(site, LAT)
    coord_y = lax.rem(lax.div(site, LAT), LAT)
    coord_z = lax.div(site, LAT * LAT)
    wavenum = (rows[0] * coord_x + rows[1] * coord_y + rows[2] * coord_z) & (LAT - 1)
    quadrant = (wavenum + LAT // 8) >> 3
    x = (wavenum - quadrant * (LAT // 4)).astype(F32) * (TURN / LAT)
    y = x * x
    sin = x * (1 + y * (-1 / 6 + y * (1 / 120 + y * (-1 / 5040 + y * (1 / 362880)))))
    cos = 1 + y * (-1 / 2 + y * (1 / 24 + y * (-1 / 720 + y * (1 / 40320 + y * (-1 / 3628800)))))
    odd = (quadrant & 1) == 1
    cos_all = jnp.where(odd, sin, cos)
    sin_all = jnp.where(odd, cos, sin)
    cos_all = jnp.where(((quadrant + 1) & 2) == 2, -cos_all, cos_all)
    sin_all = jnp.where((quadrant & 2) == 2, -sin_all, sin_all)
    return cos_all, sin_all


def kernel(
    dims, eig, momenta, pairs, slots, tau, out,
    cos_tab, sin_tab, turned, part, arrived, sinks, sources, right, half,
    rs_send, rs_recv, z_send, z_recv, own_send, own_recv, core_send, core_recv, fwd_send, fwd_recv,
    *gathered,
):
    n_t, n_x, n_p, chunks, site_count, colours = dims
    group = n_x * n_p
    slices = eig.shape[0]
    moms = momenta.shape[1]
    pair_count, vectors = tau.shape[0], tau.shape[1]
    width = 2 * vectors
    spins = tau.shape[2] // width
    per = moms // chunks
    share = vectors // group
    rows = per * share
    t, sx, sp = lax.axis_index("tm"), lax.axis_index("space"), lax.axis_index("spin")
    pos = sx * n_p + sp

    lane = lax.broadcasted_iota(jnp.int32, (1, width), 1)
    minus_first = jnp.where(lane < vectors, -1.0, 1.0).astype(F32)

    def swap(block):
        return pltpu.roll(block, vectors, 1)

    def peer(d):
        other = lax.rem(pos + d, group)
        return other, {"space": lax.div(other, n_p), "spin": lax.rem(other, n_p)}

    cos_value, sin_value = phase_tables(momenta, pos * site_count, site_count, moms)
    cos_tab[...] = cos_value
    sin_tab[...] = sin_value

    step = 16

    def compute(ch):
        def block(i, carry):
            s0 = pl.multiple_of(i * step, step)
            c_rows = cos_tab[pl.ds(s0, step), :]
            s_rows = sin_tab[pl.ds(s0, step), :]
            values = []
            for r in range(slices):
                for c in range(colours):
                    v = eig[r, pl.ds(c * site_count + s0, step), :].astype(F32)
                    values.append((r, c, v, swap(v) * minus_first))
            for mi in range(per):
                m = ch * per + mi
                cb = jnp.broadcast_to(c_rows[:, m : m + 1], (step, width))
                sb = jnp.broadcast_to(s_rows[:, m : m + 1], (step, width))
                for r, c, v, j in values:
                    turned[r, pl.ds(c * site_count + s0, step), mi * width : (mi + 1) * width] = (
                        cb * v + sb * j
                    ).astype(BF16)
            return carry

        lax.fori_loop(0, site_count // step, block, 0)
        for r in range(slices):
            product = lax.dot_general(
                eig[r], turned[r], (((0,), (0,)), ((), ())), preferred_element_type=F32
            )
            for mi in range(per):
                top = product[:vectors, mi * width : (mi + 1) * width]
                low = product[vectors:, mi * width : (mi + 1) * width]
                value = (top - swap(low) * minus_first).astype(BF16)
                for g in range(group):
                    part[ch, g, pl.ds(r * rows + mi * share, share), :] = value[g * share : (g + 1) * share]

    def rs_copies(ch):
        copies = []
        for d in range(1, group):
            other, where = peer(d)
            copies.append(pltpu.make_async_remote_copy(
                src_ref=part.at[ch, other], dst_ref=arrived.at[ch, d - 1],
                send_sem=rs_send.at[ch, d - 1], recv_sem=rs_recv.at[ch, d - 1],
                device_id=where, device_id_type=MESH))
        return copies

    def z_copies(ch):
        own = gathered[ch].at[pl.ds(t * slices, slices)]
        return [
            pltpu.make_async_remote_copy(
                src_ref=own, dst_ref=own,
                send_sem=z_send.at[ch, d - 1], recv_sem=z_recv.at[ch, d - 1],
                device_id={"tm": lax.rem(t + d, n_t)}, device_id_type=MESH)
            for d in range(1, n_t)
        ]

    def own_copies(ch):
        own = sources.at[ch, pos]
        across = [
            pltpu.make_async_remote_copy(
                src_ref=own, dst_ref=own,
                send_sem=own_send.at[ch, d - 1], recv_sem=own_recv.at[ch, d - 1],
                device_id={"space": lax.rem(sx + d, n_x)}, device_id_type=MESH)
            for d in range(1, n_x)
        ]
        core = [
            pltpu.make_async_remote_copy(
                src_ref=own, dst_ref=own,
                send_sem=core_send.at[ch, e - 1], recv_sem=core_recv.at[ch, e - 1],
                device_id={"spin": lax.rem(sp + e, n_p)}, device_id_type=MESH)
            for e in range(1, n_p)
        ]
        return across, core

    def forward_copies(ch, d):
        from_pos = lax.rem(sx + n_x - d, n_x) * n_p + sp
        block = sources.at[ch, from_pos]
        return [
            pltpu.make_async_remote_copy(
                src_ref=block, dst_ref=block,
                send_sem=fwd_send.at[ch, d - 1, e - 1], recv_sem=fwd_recv.at[ch, d - 1, e - 1],
                device_id={"spin": lax.rem(sp + e, n_p)}, device_id_type=MESH)
            for e in range(1, n_p)
        ]

    def reduce_share(ch):
        total = part[ch, pos].astype(F32)
        for d in range(1, group):
            total = total + arrived[ch, d - 1].astype(F32)
        gathered[ch][pl.ds(t * slices, slices)] = total.astype(BF16).reshape(slices, rows, width)

    def select(ch):
        for k in range(pair_count):
            sinks[ch, k] = gathered[ch][slots[pairs[0, k]]]
            sources[ch, pos, k] = gathered[ch][slots[pairs[1, k]]]

    def prepare(k, carry):
        right[k, :vectors, :] = tau[k]
        for g in range(spins):
            block = tau[k, :, g * width : (g + 1) * width].astype(F32)
            right[k, vectors:, g * width : (g + 1) * width] = (swap(block) * minus_first).astype(BF16)
        return carry

    def contract(ch):
        def pair(k, carry):
            halfway = jnp.dot(sinks[ch, k], right[k], preferred_element_type=F32)
            for g in range(spins):
                half[pl.ds(g, rows, stride=spins), :] = halfway[:, g * width : (g + 1) * width]
            for mi in range(per):
                q = jnp.concatenate(
                    [sources[ch, g, k, mi * share : (mi + 1) * share, :] for g in range(group)], axis=0)
                swapped = (swap(q.astype(F32)) * minus_first).astype(BF16)
                conjugate = jnp.concatenate([q, swapped], axis=0)
                left = half[mi * share * spins : (mi + 1) * share * spins, :].astype(BF16)
                loops = lax.dot_general(
                    left, conjugate, (((1,), (1,)), ((), ())), preferred_element_type=F32)
                out[k, ch * per + mi] = loops.astype(BF16)
            return carry

        lax.fori_loop(0, pair_count, pair, 0)

    rs, zs, owns, fwds = {}, {}, {}, {}
    barrier = pltpu.get_barrier_semaphore()
    for d in range(1, group):
        pl.semaphore_signal(barrier, inc=1, device_id=peer(d)[1], device_id_type=MESH)
    for d in range(1, n_t):
        pl.semaphore_signal(barrier, inc=1, device_id={"tm": lax.rem(t + d, n_t)}, device_id_type=MESH)
    for ch in range(chunks):
        compute(ch)
        if ch == 0:
            pl.semaphore_wait(barrier, group - 1 + n_t - 1)
        rs[ch] = rs_copies(ch)
        for copy in rs[ch]:
            copy.start()
        if ch >= 1:
            for copy in rs[ch - 1]:
                copy.wait_recv()
            reduce_share(ch - 1)
            zs[ch - 1] = z_copies(ch - 1)
            for copy in zs[ch - 1]:
                copy.start()
    lax.fori_loop(0, pair_count, prepare, 0)
    last = chunks - 1
    for copy in rs[last]:
        copy.wait_recv()
    reduce_share(last)
    zs[last] = z_copies(last)
    for copy in zs[last]:
        copy.start()
    for ch in range(chunks):
        for copy in zs[ch]:
            copy.wait_recv()
        select(ch)
        owns[ch] = own_copies(ch)
        for copy in owns[ch][0] + owns[ch][1]:
            copy.start()
    for ch in range(chunks):
        fwds[ch] = []
        for d in range(1, n_x):
            owns[ch][0][d - 1].wait_recv()
            fwds[ch].append(forward_copies(ch, d))
            for copy in fwds[ch][-1]:
                copy.start()
    for ch in range(chunks):
        for copy in owns[ch][1]:
            copy.wait_recv()
        for group_copies in fwds[ch]:
            for copy in group_copies:
                copy.wait_recv()
        contract(ch)
    for ch in range(chunks):
        for copy in rs[ch] + zs[ch] + owns[ch][0] + owns[ch][1]:
            copy.wait_send()
        for group_copies in fwds[ch]:
            for copy in group_copies:
                copy.wait_send()


CHUNKS = 2


def per_device(eigenvectors, momenta, time_pairs, slot_map, perambulators):
    n_t, n_x, n_p = lax.axis_size("tm"), lax.axis_size("space"), lax.axis_size("spin")
    group = n_x * n_p
    slices, site_count, colours, width = eigenvectors.shape
    moms = momenta.shape[0]
    pair_count, vectors, columns = perambulators.shape
    spins = columns // width
    share = vectors // group
    per = moms // CHUNKS
    rows = per * share
    eig = jnp.transpose(eigenvectors, (0, 2, 1, 3)).reshape(slices, colours * site_count, width)
    vmem = pl.BlockSpec(memory_space=pltpu.VMEM)
    smem = pl.BlockSpec(memory_space=pltpu.SMEM)
    dma = pltpu.SemaphoreType.DMA
    out = pl.pallas_call(
        functools.partial(kernel, (n_t, n_x, n_p, CHUNKS, site_count, colours)),
        out_shape=jax.ShapeDtypeStruct((pair_count, moms, share * spins, width), BF16),
        in_specs=[vmem, smem, smem, smem, vmem],
        out_specs=vmem,
        scratch_shapes=[
            pltpu.VMEM((site_count, 128), F32),
            pltpu.VMEM((site_count, 128), F32),
            pltpu.VMEM((slices, colours * site_count, per * width), BF16),
            pltpu.VMEM((CHUNKS, group, slices * rows, width), BF16),
            pltpu.VMEM((CHUNKS, group - 1, slices * rows, width), BF16),
            pltpu.VMEM((CHUNKS, pair_count, rows, width), BF16),
            pltpu.VMEM((CHUNKS, group, pair_count, rows, width), BF16),
            pltpu.VMEM((pair_count, width, columns), BF16),
            pltpu.VMEM((rows * spins, width), F32),
            dma((CHUNKS, group - 1)), dma((CHUNKS, group - 1)),
            dma((CHUNKS, n_t - 1)), dma((CHUNKS, n_t - 1)),
            dma((CHUNKS, n_x - 1)), dma((CHUNKS, n_x - 1)),
            dma((CHUNKS, n_p - 1)), dma((CHUNKS, n_p - 1)),
            dma((CHUNKS, n_x - 1, n_p - 1)), dma((CHUNKS, n_x - 1, n_p - 1)),
        ] + [pltpu.VMEM((n_t * slices, rows, width), BF16)] * CHUNKS,
        compiler_params=pltpu.CompilerParams(
            collective_id=0, has_side_effects=True, vmem_limit_bytes=40 * 1024 * 1024),
    )(eig, momenta.T, time_pairs.T, slot_map, perambulators)
    return out.reshape(pair_count, moms, share, spins, width)


def solution(mesh):
    placed = (
        P(("cfg", "tm"), ("space", "spin"), None, None),
        P(),
        P(("cfg", "tm"), None),
        P(),
        P(("cfg", "tm"), None, None),
    )
    return jax.shard_map(
        per_device,
        mesh=mesh,
        in_specs=placed,
        out_specs=P(("cfg", "tm"), None, ("space", "spin"), None, None),
        check_vma=False,
    )
```

```python
import functools

import jax
import jax.numpy as jnp
from jax import lax
from jax.experimental import pallas as pl
from jax.experimental.pallas import tpu as pltpu
from jax.sharding import PartitionSpec as P

LAT = 32
TURN = 6.283185307179586
BF16 = jnp.bfloat16
F32 = jnp.float32
MESH = pl.DeviceIdType.MESH


def phase_tables(momenta, first_site, site_count, moms):
    shape = (site_count, 128)
    lane = lax.broadcasted_iota(jnp.int32, (1, 128), 1)
    rows = []
    for axis in range(3):
        row = jnp.zeros((1, 128), jnp.int32)
        for m in range(moms):
            row = jnp.where(lane == m, momenta[axis, m], row)
        rows.append(row)
    site = first_site + lax.broadcasted_iota(jnp.int32, shape, 0)
    coord_x = lax.rem(site, LAT)
    coord_y = lax.rem(lax.div(site, LAT), LAT)
    coord_z = lax.div(site, LAT * LAT)
    wavenum = (rows[0] * coord_x + rows[1] * coord_y + rows[2] * coord_z) & (LAT - 1)
    quadrant = (wavenum + LAT // 8) >> 3
    x = (wavenum - quadrant * (LAT // 4)).astype(F32) * (TURN / LAT)
    y = x * x
    sin = x * (1 + y * (-1 / 6 + y * (1 / 120 + y * (-1 / 5040 + y * (1 / 362880)))))
    cos = 1 + y * (-1 / 2 + y * (1 / 24 + y * (-1 / 720 + y * (1 / 40320 + y * (-1 / 3628800)))))
    odd = (quadrant & 1) == 1
    cos_all = jnp.where(odd, sin, cos)
    sin_all = jnp.where(odd, cos, sin)
    cos_all = jnp.where(((quadrant + 1) & 2) == 2, -cos_all, cos_all)
    sin_all = jnp.where((quadrant & 2) == 2, -sin_all, sin_all)
    return cos_all, sin_all


def kernel(
    dims, eig_hbm, momenta_hbm, pairs_hbm, slots_hbm, sinks, sources,
    eig, momenta, pairs, slots, in_sem,
    cos_tab, sin_tab, turned, part, arrived,
    rs_send, rs_recv, z_send, z_recv, own_send, own_recv, core_send, core_recv, fwd_send, fwd_recv,
    *gathered,
):
    n_t, n_x, n_p, chunks, site_count, colours = dims
    fetches = [
        pltpu.make_async_copy(source, target, in_sem.at[index])
        for index, (source, target) in enumerate((
            (momenta_hbm, momenta), (eig_hbm, eig), (pairs_hbm, pairs), (slots_hbm, slots)))
    ]
    for fetch in fetches:
        fetch.start()
    group = n_x * n_p
    slices = eig.shape[0]
    moms = momenta.shape[1]
    pair_count, width = pairs.shape[1], eig.shape[2]
    vectors = width // 2
    per = moms // chunks
    share = vectors // group
    rows = per * share
    t, sx, sp = lax.axis_index("tm"), lax.axis_index("space"), lax.axis_index("spin")
    pos = sx * n_p + sp

    lane = lax.broadcasted_iota(jnp.int32, (1, width), 1)
    minus_first = jnp.where(lane < vectors, -1.0, 1.0).astype(F32)

    def swap(block):
        return pltpu.roll(block, vectors, 1)

    def peer(d):
        other = lax.rem(pos + d, group)
        return other, {"space": lax.div(other, n_p), "spin": lax.rem(other, n_p)}

    fetches[0].wait()
    cos_value, sin_value = phase_tables(momenta, pos * site_count, site_count, moms)
    cos_tab[...] = cos_value
    sin_tab[...] = sin_value

    step = 16

    def compute(ch):
        def block(i, carry):
            s0 = pl.multiple_of(i * step, step)
            c_rows = cos_tab[pl.ds(s0, step), :]
            s_rows = sin_tab[pl.ds(s0, step), :]
            values = []
            for r in range(slices):
                for c in range(colours):
                    v = eig[r, pl.ds(c * site_count + s0, step), :].astype(F32)
                    values.append((r, c, v, swap(v) * minus_first))
            for mi in range(per):
                m = ch * per + mi
                cb = jnp.broadcast_to(c_rows[:, m : m + 1], (step, width))
                sb = jnp.broadcast_to(s_rows[:, m : m + 1], (step, width))
                for r, c, v, j in values:
                    turned[r, pl.ds(c * site_count + s0, step), mi * width : (mi + 1) * width] = (
                        cb * v + sb * j
                    ).astype(BF16)
            return carry

        lax.fori_loop(0, site_count // step, block, 0)
        for r in range(slices):
            product = lax.dot_general(
                eig[r], turned[r], (((0,), (0,)), ((), ())), preferred_element_type=F32
            )
            for mi in range(per):
                top = product[:vectors, mi * width : (mi + 1) * width]
                low = product[vectors:, mi * width : (mi + 1) * width]
                value = (top - swap(low) * minus_first).astype(BF16)
                for g in range(group):
                    part[ch, g, pl.ds(r * rows + mi * share, share), :] = value[g * share : (g + 1) * share]

    def rs_copies(ch):
        copies = []
        for d in range(1, group):
            other, where = peer(d)
            copies.append(pltpu.make_async_remote_copy(
                src_ref=part.at[ch, other], dst_ref=arrived.at[ch, d - 1],
                send_sem=rs_send.at[ch, d - 1], recv_sem=rs_recv.at[ch, d - 1],
                device_id=where, device_id_type=MESH))
        return copies

    def z_copies(ch):
        own = gathered[ch].at[pl.ds(t * slices, slices)]
        return [
            pltpu.make_async_remote_copy(
                src_ref=own, dst_ref=own,
                send_sem=z_send.at[ch, d - 1], recv_sem=z_recv.at[ch, d - 1],
                device_id={"tm": lax.rem(t + d, n_t)}, device_id_type=MESH)
            for d in range(1, n_t)
        ]

    def own_copies(ch):
        own = sources.at[ch, pos]
        across = [
            pltpu.make_async_remote_copy(
                src_ref=own, dst_ref=own,
                send_sem=own_send.at[ch, d - 1], recv_sem=own_recv.at[ch, d - 1],
                device_id={"space": lax.rem(sx + d, n_x)}, device_id_type=MESH)
            for d in range(1, n_x)
        ]
        core = [
            pltpu.make_async_remote_copy(
                src_ref=own, dst_ref=own,
                send_sem=core_send.at[ch, e - 1], recv_sem=core_recv.at[ch, e - 1],
                device_id={"spin": lax.rem(sp + e, n_p)}, device_id_type=MESH)
            for e in range(1, n_p)
        ]
        return across, core

    def forward_copies(ch, d):
        from_pos = lax.rem(sx + n_x - d, n_x) * n_p + sp
        block = sources.at[ch, from_pos]
        return [
            pltpu.make_async_remote_copy(
                src_ref=block, dst_ref=block,
                send_sem=fwd_send.at[ch, d - 1, e - 1], recv_sem=fwd_recv.at[ch, d - 1, e - 1],
                device_id={"spin": lax.rem(sp + e, n_p)}, device_id_type=MESH)
            for e in range(1, n_p)
        ]

    def reduce_share(ch):
        total = part[ch, pos].astype(F32)
        for d in range(1, group):
            total = total + arrived[ch, d - 1].astype(F32)
        gathered[ch][pl.ds(t * slices, slices)] = total.astype(BF16).reshape(slices, rows, width)

    def select(ch):
        for k in range(pair_count):
            sinks[ch, k] = gathered[ch][slots[pairs[0, k]]]
            sources[ch, pos, k] = gathered[ch][slots[pairs[1, k]]]

    rs, zs, owns, fwds = {}, {}, {}, {}
    barrier = pltpu.get_barrier_semaphore()
    for d in range(1, group):
        pl.semaphore_signal(barrier, inc=1, device_id=peer(d)[1], device_id_type=MESH)
    for d in range(1, n_t):
        pl.semaphore_signal(barrier, inc=1, device_id={"tm": lax.rem(t + d, n_t)}, device_id_type=MESH)
    fetches[1].wait()

    def reduced(ch):
        for copy in rs[ch]:
            copy.wait_recv()
        reduce_share(ch)
        zs[ch] = z_copies(ch)
        for copy in zs[ch]:
            copy.start()

    def selected(ch):
        if ch == 0:
            for fetch in fetches[2:]:
                fetch.wait()
        for copy in zs[ch]:
            copy.wait_recv()
        select(ch)
        owns[ch] = own_copies(ch)
        for copy in owns[ch][0] + owns[ch][1]:
            copy.start()

    def forwarded(ch):
        fwds[ch] = []
        for d in range(1, n_x):
            owns[ch][0][d - 1].wait_recv()
            fwds[ch].append(forward_copies(ch, d))
            for copy in fwds[ch][-1]:
                copy.start()

    for ch in range(chunks):
        compute(ch)
        if ch == 0:
            pl.semaphore_wait(barrier, group - 1 + n_t - 1)
        rs[ch] = rs_copies(ch)
        for copy in rs[ch]:
            copy.start()
        if ch >= 1:
            reduced(ch - 1)
        if ch >= 3:
            selected(ch - 3)
    reduced(chunks - 1)
    for ch in range(max(chunks - 3, 0), chunks):
        selected(ch)
        if ch >= 1:
            forwarded(ch - 1)
    forwarded(chunks - 1)
    for ch in range(chunks):
        for copy in owns[ch][1]:
            copy.wait_recv()
        for group_copies in fwds[ch]:
            for copy in group_copies:
                copy.wait_recv()
    for ch in range(chunks):
        for copy in rs[ch] + zs[ch] + owns[ch][0] + owns[ch][1]:
            copy.wait_send()
        for group_copies in fwds[ch]:
            for copy in group_copies:
                copy.wait_send()


def contraction(sinks, sources, tau, out, right, half):
    chunks, group, rows, width = sources.shape[0], sources.shape[1], sources.shape[3], sources.shape[4]
    vectors = width // 2
    spins = tau.shape[2] // width
    share = vectors // group
    per = rows // share
    lane = lax.broadcasted_iota(jnp.int32, (1, width), 1)
    minus_first = jnp.where(lane < vectors, -1.0, 1.0).astype(F32)

    right[:vectors, :] = tau[0]
    for g in range(spins):
        block = tau[0, :, g * width : (g + 1) * width].astype(F32)
        right[vectors:, g * width : (g + 1) * width] = (
            pltpu.roll(block, vectors, 1) * minus_first).astype(BF16)
    left = sinks[:, 0].reshape(chunks * rows, width)
    for g in range(0, spins, 2):
        halfway = jnp.dot(left, right[:, g * width : (g + 2) * width], preferred_element_type=F32)
        for e in range(2):
            half[pl.ds(g + e, chunks * rows, stride=spins), :] = halfway[:, e * width : (e + 1) * width]
    block_rows = share * spins
    for ch in range(chunks):
        for mi in range(per):
            m = ch * per + mi
            q = jnp.concatenate(
                [sources[ch, g, 0, mi * share : (mi + 1) * share, :] for g in range(group)], axis=0)
            swapped = (pltpu.roll(q.astype(F32), vectors, 1) * minus_first).astype(BF16)
            conjugate = jnp.concatenate([q, swapped], axis=0)
            out[0, m] = lax.dot_general(
                half[m * block_rows : (m + 1) * block_rows, :].astype(BF16), conjugate,
                (((1,), (1,)), ((), ())), preferred_element_type=F32).astype(BF16)


CHUNKS = 4


def per_device(eigenvectors, momenta, time_pairs, slot_map, perambulators):
    n_t, n_x, n_p = lax.axis_size("tm"), lax.axis_size("space"), lax.axis_size("spin")
    group = n_x * n_p
    slices, site_count, colours, width = eigenvectors.shape
    moms = momenta.shape[0]
    pair_count, vectors, columns = perambulators.shape
    spins = columns // width
    share = vectors // group
    per = moms // CHUNKS
    rows = per * share
    eig = jnp.transpose(eigenvectors, (0, 2, 1, 3)).reshape(slices, colours * site_count, width)
    vmem = pl.BlockSpec(memory_space=pltpu.VMEM)
    hbm = pl.BlockSpec(memory_space=pltpu.HBM)
    dma = pltpu.SemaphoreType.DMA
    sinks, sources = pl.pallas_call(
        functools.partial(kernel, (n_t, n_x, n_p, CHUNKS, site_count, colours)),
        out_shape=[
            jax.ShapeDtypeStruct((CHUNKS, pair_count, rows, width), BF16),
            jax.ShapeDtypeStruct((CHUNKS, group, pair_count, rows, width), BF16),
        ],
        in_specs=[hbm] * 4,
        out_specs=[vmem, vmem],
        scratch_shapes=[
            pltpu.VMEM(eig.shape, BF16),
            pltpu.SMEM((momenta.shape[1], moms), jnp.int32),
            pltpu.SMEM((2, pair_count), jnp.int32),
            pltpu.SMEM(slot_map.shape, jnp.int32),
            dma((4,)),
            pltpu.VMEM((site_count, 128), F32),
            pltpu.VMEM((site_count, 128), F32),
            pltpu.VMEM((slices, colours * site_count, per * width), BF16),
            pltpu.VMEM((CHUNKS, group, slices * rows, width), BF16),
            pltpu.VMEM((CHUNKS, group - 1, slices * rows, width), BF16),
            dma((CHUNKS, group - 1)), dma((CHUNKS, group - 1)),
            dma((CHUNKS, n_t - 1)), dma((CHUNKS, n_t - 1)),
            dma((CHUNKS, n_x - 1)), dma((CHUNKS, n_x - 1)),
            dma((CHUNKS, n_p - 1)), dma((CHUNKS, n_p - 1)),
            dma((CHUNKS, n_x - 1, n_p - 1)), dma((CHUNKS, n_x - 1, n_p - 1)),
        ] + [pltpu.VMEM((n_t * slices, rows, width), BF16)] * CHUNKS,
        compiler_params=pltpu.CompilerParams(
            collective_id=0, has_side_effects=True, vmem_limit_bytes=VMEM_MIB * 1024 * 1024),
    )(eig, momenta.T, time_pairs.T, slot_map)
    out = pl.pallas_call(
        contraction,
        grid=(pair_count,),
        out_shape=jax.ShapeDtypeStruct((pair_count, moms, share * spins, width), BF16),
        in_specs=[
            pl.BlockSpec((CHUNKS, 1, rows, width), lambda k: (0, k, 0, 0)),
            pl.BlockSpec((CHUNKS, group, 1, rows, width), lambda k: (0, 0, k, 0, 0)),
            pl.BlockSpec((1, vectors, columns), lambda k: (k, 0, 0)),
        ],
        out_specs=pl.BlockSpec((1, moms, share * spins, width), lambda k: (k, 0, 0, 0)),
        scratch_shapes=[
            pltpu.VMEM((width, columns), BF16),
            pltpu.VMEM((moms * share * spins, width), F32),
        ],
        compiler_params=pltpu.CompilerParams(vmem_limit_bytes=VMEM_MIB * 1024 * 1024),
    )(sinks, sources, perambulators)
    return out.reshape(pair_count, moms, share, spins, width)


VMEM_MIB = 63


def solution(mesh):
    placed = (
        P(("cfg", "tm"), ("space", "spin"), None, None),
        P(),
        P(("cfg", "tm"), None),
        P(),
        P(("cfg", "tm"), None, None),
    )
    return jax.shard_map(
        per_device,
        mesh=mesh,
        in_specs=placed,
        out_specs=P(("cfg", "tm"), None, ("space", "spin"), None, None),
        check_vma=False,
    )
```

```python
import functools

import jax
import jax.numpy as jnp
from jax import lax
from jax.experimental import pallas as pl
from jax.experimental.pallas import tpu as pltpu
from jax.sharding import PartitionSpec as P

LAT = 32
TURN = 6.283185307179586
BF16 = jnp.bfloat16
F32 = jnp.float32
MESH = pl.DeviceIdType.MESH


def phase_tables(momenta, first_site, site_count, moms):
    shape = (site_count, 128)
    lane = lax.broadcasted_iota(jnp.int32, (1, 128), 1)
    rows = []
    for axis in range(3):
        row = jnp.zeros((1, 128), jnp.int32)
        for m in range(moms):
            row = jnp.where(lane == m, momenta[axis, m], row)
        rows.append(row)
    site = first_site + lax.broadcasted_iota(jnp.int32, shape, 0)
    coord_x = lax.rem(site, LAT)
    coord_y = lax.rem(lax.div(site, LAT), LAT)
    coord_z = lax.div(site, LAT * LAT)
    wavenum = (rows[0] * coord_x + rows[1] * coord_y + rows[2] * coord_z) & (LAT - 1)
    quadrant = (wavenum + LAT // 8) >> 3
    x = (wavenum - quadrant * (LAT // 4)).astype(F32) * (TURN / LAT)
    y = x * x
    sin = x * (1 + y * (-1 / 6 + y * (1 / 120 + y * (-1 / 5040 + y * (1 / 362880)))))
    cos = 1 + y * (-1 / 2 + y * (1 / 24 + y * (-1 / 720 + y * (1 / 40320 + y * (-1 / 3628800)))))
    odd = (quadrant & 1) == 1
    cos_all = jnp.where(odd, sin, cos)
    sin_all = jnp.where(odd, cos, sin)
    cos_all = jnp.where(((quadrant + 1) & 2) == 2, -cos_all, cos_all)
    sin_all = jnp.where((quadrant & 2) == 2, -sin_all, sin_all)
    return cos_all, sin_all


def kernel(
    dims, eig_hbm, momenta_hbm, pairs_hbm, slots_hbm, sinks, sources,
    eig, momenta, pairs, slots, in_sem,
    cos_tab, sin_tab, turned, part, arrived,
    rs_send, rs_recv, z_send, z_recv, own_send, own_recv, core_send, core_recv, fwd_send, fwd_recv,
    *gathered,
):
    n_t, n_x, n_p, chunks, site_count, colours = dims
    fetches = [
        pltpu.make_async_copy(source, target, in_sem.at[index])
        for index, (source, target) in enumerate((
            (momenta_hbm, momenta), (eig_hbm, eig), (pairs_hbm, pairs), (slots_hbm, slots)))
    ]
    for fetch in fetches:
        fetch.start()
    group = n_x * n_p
    slices = eig.shape[0]
    moms = momenta.shape[1]
    pair_count, width = pairs.shape[1], eig.shape[2]
    vectors = width // 2
    per = moms // chunks
    share = vectors // group
    rows = per * share
    t, sx, sp = lax.axis_index("tm"), lax.axis_index("space"), lax.axis_index("spin")
    pos = sx * n_p + sp

    lane = lax.broadcasted_iota(jnp.int32, (1, width), 1)
    minus_first = jnp.where(lane < vectors, -1.0, 1.0).astype(F32)

    def swap(block):
        return pltpu.roll(block, vectors, 1)

    def peer(d):
        other = lax.rem(pos + d, group)
        return other, {"space": lax.div(other, n_p), "spin": lax.rem(other, n_p)}

    fetches[0].wait()
    cos_value, sin_value = phase_tables(momenta, pos * site_count, site_count, moms)
    cos_tab[...] = cos_value
    sin_tab[...] = sin_value

    step = STEP

    def compute(ch):
        def block(i, carry):
            s0 = pl.multiple_of(i * step, step)
            c_rows = cos_tab[pl.ds(s0, step), :]
            s_rows = sin_tab[pl.ds(s0, step), :]
            values = []
            for r in range(slices):
                for c in range(colours):
                    v = eig[r, pl.ds(c * site_count + s0, step), :].astype(F32)
                    values.append((r, c, v, swap(v) * minus_first))
            for mi in range(per):
                m = ch * per + mi
                cb = jnp.broadcast_to(c_rows[:, m : m + 1], (step, width))
                sb = jnp.broadcast_to(s_rows[:, m : m + 1], (step, width))
                for r, c, v, j in values:
                    turned[r, pl.ds(c * site_count + s0, step), mi * width : (mi + 1) * width] = (
                        cb * v + sb * j
                    ).astype(BF16)
            return carry

        lax.fori_loop(0, site_count // step, block, 0, unroll=UNROLL)
        for r in range(slices):
            product = lax.dot_general(
                eig[r], turned[r], (((0,), (0,)), ((), ())), preferred_element_type=F32
            )
            for mi in range(per):
                top = product[:vectors, mi * width : (mi + 1) * width]
                low = product[vectors:, mi * width : (mi + 1) * width]
                value = (top - swap(low) * minus_first).astype(BF16)
                for g in range(group):
                    part[ch, g, pl.ds(r * rows + mi * share, share), :] = value[g * share : (g + 1) * share]

    def rs_copies(ch):
        copies = []
        for d in range(1, group):
            other, where = peer(d)
            copies.append(pltpu.make_async_remote_copy(
                src_ref=part.at[ch, other], dst_ref=arrived.at[ch, d - 1],
                send_sem=rs_send.at[ch, d - 1], recv_sem=rs_recv.at[ch, d - 1],
                device_id=where, device_id_type=MESH))
        return copies

    def z_copies(ch):
        own = gathered[ch].at[pl.ds(t * slices, slices)]
        return [
            pltpu.make_async_remote_copy(
                src_ref=own, dst_ref=own,
                send_sem=z_send.at[ch, d - 1], recv_sem=z_recv.at[ch, d - 1],
                device_id={"tm": lax.rem(t + d, n_t)}, device_id_type=MESH)
            for d in range(1, n_t)
        ]

    def own_copies(ch):
        own = sources.at[ch, pos]
        across = [
            pltpu.make_async_remote_copy(
                src_ref=own, dst_ref=own,
                send_sem=own_send.at[ch, d - 1], recv_sem=own_recv.at[ch, d - 1],
                device_id={"space": lax.rem(sx + d, n_x)}, device_id_type=MESH)
            for d in range(1, n_x)
        ]
        core = [
            pltpu.make_async_remote_copy(
                src_ref=own, dst_ref=own,
                send_sem=core_send.at[ch, e - 1], recv_sem=core_recv.at[ch, e - 1],
                device_id={"spin": lax.rem(sp + e, n_p)}, device_id_type=MESH)
            for e in range(1, n_p)
        ]
        return across, core

    def forward_copies(ch, d):
        from_pos = lax.rem(sx + n_x - d, n_x) * n_p + sp
        block = sources.at[ch, from_pos]
        return [
            pltpu.make_async_remote_copy(
                src_ref=block, dst_ref=block,
                send_sem=fwd_send.at[ch, d - 1, e - 1], recv_sem=fwd_recv.at[ch, d - 1, e - 1],
                device_id={"spin": lax.rem(sp + e, n_p)}, device_id_type=MESH)
            for e in range(1, n_p)
        ]

    def reduce_share(ch):
        total = part[ch, pos].astype(F32)
        for d in range(1, group):
            total = total + arrived[ch, d - 1].astype(F32)
        gathered[ch][pl.ds(t * slices, slices)] = total.astype(BF16).reshape(slices, rows, width)

    def select(ch):
        for k in range(pair_count):
            sinks[ch, k] = gathered[ch][slots[pairs[0, k]]]
            sources[ch, pos, k] = gathered[ch][slots[pairs[1, k]]]

    rs, zs, owns, fwds = {}, {}, {}, {}
    barrier = pltpu.get_barrier_semaphore()
    for d in range(1, group):
        pl.semaphore_signal(barrier, inc=1, device_id=peer(d)[1], device_id_type=MESH)
    for d in range(1, n_t):
        pl.semaphore_signal(barrier, inc=1, device_id={"tm": lax.rem(t + d, n_t)}, device_id_type=MESH)
    fetches[1].wait()

    def reduced(ch):
        for copy in rs[ch]:
            copy.wait_recv()
        reduce_share(ch)
        zs[ch] = z_copies(ch)
        for copy in zs[ch]:
            copy.start()

    def selected(ch):
        if ch == 0:
            for fetch in fetches[2:]:
                fetch.wait()
        for copy in zs[ch]:
            copy.wait_recv()
        select(ch)
        owns[ch] = own_copies(ch)
        for copy in owns[ch][0] + owns[ch][1]:
            copy.start()

    def forwarded(ch):
        fwds[ch] = []
        for d in range(1, n_x):
            owns[ch][0][d - 1].wait_recv()
            fwds[ch].append(forward_copies(ch, d))
            for copy in fwds[ch][-1]:
                copy.start()

    for ch in range(chunks):
        compute(ch)
        if ch == 0:
            pl.semaphore_wait(barrier, group - 1 + n_t - 1)
        rs[ch] = rs_copies(ch)
        for copy in rs[ch]:
            copy.start()
        if ch >= 1:
            reduced(ch - 1)
        if ch >= 3:
            selected(ch - 3)
    reduced(chunks - 1)
    for ch in range(max(chunks - 3, 0), chunks):
        selected(ch)
        if ch >= 1:
            forwarded(ch - 1)
    forwarded(chunks - 1)
    for ch in range(chunks):
        for copy in owns[ch][1]:
            copy.wait_recv()
        for group_copies in fwds[ch]:
            for copy in group_copies:
                copy.wait_recv()
    for ch in range(chunks):
        for copy in rs[ch] + zs[ch] + owns[ch][0] + owns[ch][1]:
            copy.wait_send()
        for group_copies in fwds[ch]:
            for copy in group_copies:
                copy.wait_send()


def contraction(sinks, sources, tau, out, right, half):
    chunks, group, rows, width = sources.shape[0], sources.shape[1], sources.shape[3], sources.shape[4]
    vectors = width // 2
    spins = tau.shape[2] // width
    share = vectors // group
    per = rows // share
    lane = lax.broadcasted_iota(jnp.int32, (1, width), 1)
    minus_first = jnp.where(lane < vectors, -1.0, 1.0).astype(F32)

    right[:vectors, :] = tau[0]
    for g in range(spins):
        block = tau[0, :, g * width : (g + 1) * width].astype(F32)
        right[vectors:, g * width : (g + 1) * width] = (
            pltpu.roll(block, vectors, 1) * minus_first).astype(BF16)
    left = sinks[:, 0].reshape(chunks * rows, width)
    for g in range(0, spins, 2):
        halfway = jnp.dot(left, right[:, g * width : (g + 2) * width], preferred_element_type=F32)
        for e in range(2):
            half[pl.ds(g + e, chunks * rows, stride=spins), :] = halfway[:, e * width : (e + 1) * width]
    block_rows = share * spins
    for ch in range(chunks):
        for mi in range(per):
            m = ch * per + mi
            q = jnp.concatenate(
                [sources[ch, g, 0, mi * share : (mi + 1) * share, :] for g in range(group)], axis=0)
            swapped = (pltpu.roll(q.astype(F32), vectors, 1) * minus_first).astype(BF16)
            conjugate = jnp.concatenate([q, swapped], axis=0)
            out[0, m] = lax.dot_general(
                half[m * block_rows : (m + 1) * block_rows, :].astype(BF16), conjugate,
                (((1,), (1,)), ((), ())), preferred_element_type=F32).astype(BF16)


CHUNKS = 2
STEP = 16
UNROLL = 8


def per_device(eigenvectors, momenta, time_pairs, slot_map, perambulators):
    n_t, n_x, n_p = lax.axis_size("tm"), lax.axis_size("space"), lax.axis_size("spin")
    group = n_x * n_p
    slices, site_count, colours, width = eigenvectors.shape
    moms = momenta.shape[0]
    pair_count, vectors, columns = perambulators.shape
    spins = columns // width
    share = vectors // group
    per = moms // CHUNKS
    rows = per * share
    eig = jnp.transpose(eigenvectors, (0, 2, 1, 3)).reshape(slices, colours * site_count, width)
    vmem = pl.BlockSpec(memory_space=pltpu.VMEM)
    hbm = pl.BlockSpec(memory_space=pltpu.HBM)
    dma = pltpu.SemaphoreType.DMA
    sinks, sources = pl.pallas_call(
        functools.partial(kernel, (n_t, n_x, n_p, CHUNKS, site_count, colours)),
        out_shape=[
            jax.ShapeDtypeStruct((CHUNKS, pair_count, rows, width), BF16),
            jax.ShapeDtypeStruct((CHUNKS, group, pair_count, rows, width), BF16),
        ],
        in_specs=[hbm] * 4,
        out_specs=[vmem, vmem],
        scratch_shapes=[
            pltpu.VMEM(eig.shape, BF16),
            pltpu.SMEM((momenta.shape[1], moms), jnp.int32),
            pltpu.SMEM((2, pair_count), jnp.int32),
            pltpu.SMEM(slot_map.shape, jnp.int32),
            dma((4,)),
            pltpu.VMEM((site_count, 128), F32),
            pltpu.VMEM((site_count, 128), F32),
            pltpu.VMEM((slices, colours * site_count, per * width), BF16),
            pltpu.VMEM((CHUNKS, group, slices * rows, width), BF16),
            pltpu.VMEM((CHUNKS, group - 1, slices * rows, width), BF16),
            dma((CHUNKS, group - 1)), dma((CHUNKS, group - 1)),
            dma((CHUNKS, n_t - 1)), dma((CHUNKS, n_t - 1)),
            dma((CHUNKS, n_x - 1)), dma((CHUNKS, n_x - 1)),
            dma((CHUNKS, n_p - 1)), dma((CHUNKS, n_p - 1)),
            dma((CHUNKS, n_x - 1, n_p - 1)), dma((CHUNKS, n_x - 1, n_p - 1)),
        ] + [pltpu.VMEM((n_t * slices, rows, width), BF16)] * CHUNKS,
        compiler_params=pltpu.CompilerParams(
            collective_id=0, has_side_effects=True, vmem_limit_bytes=VMEM_MIB * 1024 * 1024),
    )(eig, momenta.T, time_pairs.T, slot_map)
    out = pl.pallas_call(
        contraction,
        grid=(pair_count,),
        out_shape=jax.ShapeDtypeStruct((pair_count, moms, share * spins, width), BF16),
        in_specs=[
            pl.BlockSpec((CHUNKS, 1, rows, width), lambda k: (0, k, 0, 0)),
            pl.BlockSpec((CHUNKS, group, 1, rows, width), lambda k: (0, 0, k, 0, 0)),
            pl.BlockSpec((1, vectors, columns), lambda k: (k, 0, 0)),
        ],
        out_specs=pl.BlockSpec((1, moms, share * spins, width), lambda k: (k, 0, 0, 0)),
        scratch_shapes=[
            pltpu.VMEM((width, columns), BF16),
            pltpu.VMEM((moms * share * spins, width), F32),
        ],
        compiler_params=pltpu.CompilerParams(vmem_limit_bytes=VMEM_MIB * 1024 * 1024),
    )(sinks, sources, perambulators)
    return out.reshape(pair_count, moms, share, spins, width)


VMEM_MIB = 63


def solution(mesh):
    placed = (
        P(("cfg", "tm"), ("space", "spin"), None, None),
        P(),
        P(("cfg", "tm"), None),
        P(),
        P(("cfg", "tm"), None, None),
    )
    return jax.shard_map(
        per_device,
        mesh=mesh,
        in_specs=placed,
        out_specs=P(("cfg", "tm"), None, ("space", "spin"), None, None),
        check_vma=False,
    )
```
